32 devices in a mesh: gx: 4 (over z), gy: 2 (over x), gz: 4 (over y, core).
Axes of the slice: x: 2, y: 2, z: 4, core: 2. Of those that a mesh axis runs over, the one named last changes fastest.
Arguments:
- positions: bfloat16 [4, 2, 4, 3, 64], P('gx', 'gy', 'gz'), may hold values from 0 to 2
- features: bfloat16 [4, 2, 4, 64, 512], P('gx', 'gy', 'gz'), may hold values from -6 to 6
- ghost_lists: int32 [4, 2, 4, 3, 2, 48], P('gx', 'gy', 'gz'), may hold values from 0 to 63, as said below
- move_lists: int32 [4, 2, 4, 3, 2, 4], P('gx', 'gy', 'gz'), may hold values from 0 to 63, as said below
- neighbours: int32 [4, 2, 4, 8, 64], P('gx', 'gy', 'gz'), may hold values from 0 to 351, as said below
- w_self: bfloat16 [512, 512], replicated, may hold values from -0.25 to 0.25
- w_pair: bfloat16 [512, 512], replicated, may hold values from -0.25 to 0.25
- w_radial: float32 [8, 512], replicated, may hold values from -2 to 2
- w_mix: bfloat16 [512, 512], replicated, may hold values from -0.25 to 0.25
- w_env: bfloat16 [512, 32], replicated, may hold values from -0.25 to 0.25
- w_scal: float32 [96, 512], replicated, may hold values from -0.625 to 0.625
- w_upd: bfloat16 [512, 512], replicated, may hold values from -0.25 to 0.25
- w_out: float32 [512], replicated, may hold values from -0.25 to 0.25
Outputs:
- forces: float32 [4, 2, 4, 3, 64], P('gx', 'gy', 'gz')
- atom_energy: float32 [4, 2, 4, 64], P('gx', 'gy', 'gz')
- moved_positions: bfloat16 [4, 2, 4, 3, 64], P('gx', 'gy', 'gz')
- moved_features: bfloat16 [4, 2, 4, 64, 512], P('gx', 'gy', 'gz')
The draws below stay inside these ranges and needn't reach their ends.
Inputs may be any that keep to these rules, and one draw needn't show every extreme that they name: `ghost_lists`: each block of 48 entries names distinct atoms. `move_lists`: the 24 entries of one cell are distinct. `neighbours`: entry k of atom i never equals i.
All inputs are finite; a program needn't handle non-finite values.
Results may differ from the reference program's by a relative error of at most 0.015.
Values may be sent and summed in bfloat16 or wider, within the bound.
A program may use at most 64 MiB of HBM per device.

```python
import math
import jax
import jax.numpy as jnp
from jax import lax

LATENT = 512
CHANNELS = 32
RADIAL = 8
ATOMS = 64
NEIGH = 8
GHOSTS = 48
MOVES = 4
N_GX = 4
N_GY = 2
N_GZ = 4


def draw_ghost_lists(key, part):
    key = jax.random.fold_in(key, 11)
    subkeys = jax.random.split(key, N_GX * N_GY * N_GZ * 6)
    chosen = jax.vmap(lambda single: jax.random.permutation(single, ATOMS)[:GHOSTS])(subkeys)
    return chosen.reshape(N_GX, N_GY, N_GZ, 3, 2, GHOSTS).astype(jnp.int32)


def draw_move_lists(key, part):
    key = jax.random.fold_in(key, 17)
    subkeys = jax.random.split(key, N_GX * N_GY * N_GZ)
    chosen = jax.vmap(lambda single: jax.random.permutation(single, ATOMS)[:6 * MOVES])(subkeys)
    return chosen.reshape(N_GX, N_GY, N_GZ, 3, 2, MOVES).astype(jnp.int32)


def draw_neighbours(key, part):
    key = jax.random.fold_in(key, 23)
    drawn = jax.random.randint(key, (N_GX, N_GY, N_GZ, NEIGH, ATOMS), 0, ATOMS + 6 * GHOSTS - 1)
    owners = jnp.arange(ATOMS, dtype=jnp.int32)
    return jnp.where(drawn >= owners, drawn + 1, drawn).astype(jnp.int32)


def level_of(own_key, shape, cuts, low, high):
    def one(dim, shards_of):
        heights = jax.random.uniform(jax.random.fold_in(jax.random.fold_in(own_key, 6), dim), (shards_of,), jnp.float32, low / len(cuts), high / len(cuts))
        return jnp.repeat(jnp.exp(heights), shape[dim] // shards_of).reshape((-1,) + (1,) * (len(shape) - dim - 1))

    loudness = one(*cuts[0])
    for cut in cuts[1:]:
        loudness = loudness * one(*cut)
    return loudness


def gaussian(own_key, dims, deviation, limit, pieces=(), held_as=jnp.bfloat16):
    values = deviation * jax.random.normal(own_key, dims, jnp.float32)
    if pieces:
        values = values * level_of(own_key, dims, pieces, -0.22, 0.18)
    return jnp.clip(values, -limit, limit).astype(held_as)


def setup_inputs(seed: int = 0) -> dict:
    keys = jax.random.split(jax.random.key(seed), 14)
    return {
        "positions": jnp.clip(2.0 * jax.random.uniform(keys[0], (N_GX, N_GY, N_GZ, 3, ATOMS), jnp.float32) ** level_of(keys[0], (N_GX, N_GY, N_GZ, 3, ATOMS), ((0, 4), (1, 2), (2, 4)), -0.2, 0.2), 0.0, 2.0).astype(jnp.bfloat16),
        "features": gaussian(keys[1], (N_GX, N_GY, N_GZ, ATOMS, LATENT), 1.0, 6.0, ((0, 4), (1, 2), (2, 4))),
        "ghost_lists": draw_ghost_lists(jax.random.fold_in(keys[13], 71), 0),
        "move_lists": draw_move_lists(jax.random.fold_in(keys[13], 71), 0),
        "neighbours": draw_neighbours(jax.random.fold_in(keys[13], 71), 0),
        "w_self": gaussian(keys[5], (LATENT, LATENT), LATENT ** -0.5, 0.25),
        "w_pair": gaussian(keys[6], (LATENT, LATENT), LATENT ** -0.5, 0.25),
        "w_radial": gaussian(keys[7], (RADIAL, LATENT), RADIAL ** -0.5, 2.0, (), jnp.float32),
        "w_mix": gaussian(keys[8], (LATENT, LATENT), LATENT ** -0.5, 0.25),
        "w_env": gaussian(keys[9], (LATENT, CHANNELS), LATENT ** -0.5, 0.25),
        "w_scal": gaussian(keys[10], (3 * CHANNELS, LATENT), (3 * CHANNELS) ** -0.5, 0.625, (), jnp.float32),
        "w_upd": gaussian(keys[11], (LATENT, LATENT), LATENT ** -0.5, 0.25),
        "w_out": gaussian(keys[12], (LATENT,), LATENT ** -0.5, 0.25, (), jnp.float32),
    }


cell_edge = 2.0
basis_width = 0.5

def harmonics(unit_vec):
    ux, uy, uz = (unit_vec[0], unit_vec[1], unit_vec[2])
    root3 = math.sqrt(3.0)
    root15 = math.sqrt(15.0)
    root5 = math.sqrt(5.0)
    return jnp.stack([jnp.ones_like(ux), root3 * ux, root3 * uy, root3 * uz, root15 * ux * uy, root15 * uy * uz, 0.5 * root5 * (3.0 * uz * uz - 1.0), root15 * ux * uz, 0.5 * root15 * (ux * ux - uy * uy)])

def cell_energy(ext_pos, self_proj, ext_pair, neigh_index, w_radial, w_mix, w_env, w_scal, w_upd, w_out):
    neigh_count, atom_count = neigh_index.shape
    flat_index = neigh_index.T.reshape(-1)
    centre = jnp.repeat(ext_pos[:, :atom_count], neigh_count, axis=1)
    offset = ext_pos[:, flat_index] - centre
    distance = jnp.sqrt(lax.optimization_barrier(jnp.sum(offset * offset, axis=0)) + 0.25)
    harm = harmonics(offset / distance).T
    centers = basis_width * jnp.arange(w_radial.shape[0]).astype(jnp.float32)
    basis = jnp.exp(-jnp.square((distance[:, None] - centers[None, :]) / basis_width))
    before = jnp.repeat(self_proj, neigh_count, axis=0).astype(jnp.float32) + ext_pair[flat_index].astype(jnp.float32)
    before = before + jnp.dot(basis, w_radial, precision=lax.Precision.HIGHEST)
    latent = jax.nn.silu(before).astype(jnp.bfloat16)
    mixed = jax.nn.silu(jnp.dot(latent, w_mix, preferred_element_type=jnp.float32)).astype(jnp.bfloat16)
    env_w = jnp.dot(mixed, w_env, preferred_element_type=jnp.float32)
    channels = env_w.shape[1]
    tensor = env_w[:, :, None] * harm[:, None, :]
    environment = tensor.reshape(atom_count, neigh_count, channels, 9).sum(axis=1) / math.sqrt(neigh_count)
    project = jnp.repeat(environment, neigh_count, axis=0) * harm[:, None, :]
    invariants = jnp.concatenate([project[:, :, 0:1], lax.optimization_barrier(jnp.sum(project[:, :, 1:4], axis=2, keepdims=True)), lax.optimization_barrier(jnp.sum(project[:, :, 4:9], axis=2, keepdims=True))], axis=2)
    invariants = invariants.reshape(atom_count * neigh_count, 3 * channels)
    update = jax.nn.silu(jnp.dot(mixed, w_upd, preferred_element_type=jnp.float32) + jnp.dot(invariants, w_scal, precision=lax.Precision.HIGHEST))
    edge_energy = jnp.dot(update, w_out, precision=lax.Precision.HIGHEST)
    return edge_energy.reshape(atom_count, neigh_count).sum(axis=1)

def energy_and_gradient(ext_pos, self_proj, ext_pair, neigh_index, weights):

    def energy_of(places):
        return cell_energy(places, self_proj, ext_pair, neigh_index, *weights)
    energy, pullback = jax.vjp(energy_of, ext_pos)
    gradient = pullback(jnp.ones_like(energy))[0]
    return (energy, gradient)

def reference(positions, features, ghost_lists, move_lists, neighbours, w_self, w_pair, w_radial, w_mix, w_env, w_scal, w_upd, w_out):
    grid = positions.shape[:3]
    atom_count = positions.shape[4]
    width = features.shape[4]
    ghost_count = ghost_lists.shape[5]
    places = positions.astype(jnp.float32)
    self_proj = jnp.dot(features.reshape(-1, width), w_self, preferred_element_type=jnp.float32).astype(jnp.bfloat16).reshape(features.shape)
    pair_proj = jnp.dot(features.reshape(-1, width), w_pair, preferred_element_type=jnp.float32).astype(jnp.bfloat16).reshape(features.shape)

    def take_rows(table, chosen):
        return jnp.take_along_axis(table, chosen[..., None], axis=3)

    def take_cols(table, chosen):
        return jnp.take_along_axis(table, chosen[..., None, :], axis=4)
    pos_parts = [places]
    row_parts = [pair_proj]
    for direction in range(3):
        shift = (jnp.arange(3) == direction).astype(jnp.float32)[:, None] * cell_edge
        pos_parts.append(jnp.roll(take_cols(places, ghost_lists[:, :, :, direction, 1]), 1, axis=direction) - shift)
        pos_parts.append(jnp.roll(take_cols(places, ghost_lists[:, :, :, direction, 0]), -1, axis=direction) + shift)
        row_parts.append(jnp.roll(take_rows(pair_proj, ghost_lists[:, :, :, direction, 1]), 1, axis=direction))
        row_parts.append(jnp.roll(take_rows(pair_proj, ghost_lists[:, :, :, direction, 0]), -1, axis=direction))
    ext_pos = jnp.concatenate(pos_parts, axis=4)
    ext_pair = jnp.concatenate(row_parts, axis=3)
    ext_count = ext_pos.shape[4]
    weights = (w_radial, w_mix, w_env, w_scal, w_upd, w_out)

    def one_cell(packed):
        return energy_and_gradient(packed[0], packed[1], packed[2], packed[3], weights)
    energy, gradient = lax.map(one_cell, (ext_pos.reshape(-1, 3, ext_count), self_proj.reshape(-1, atom_count, width), ext_pair.reshape(-1, ext_count, width), neighbours.reshape(-1, neighbours.shape[3], atom_count)))
    gradient = gradient.reshape(grid + (3, ext_count))
    forces = -gradient[..., :atom_count]

    def add_at(target, chosen, values):
        return target.at[:, chosen].add(-values)
    add_cells = jax.vmap(add_at)
    flat_forces = forces.reshape(-1, 3, atom_count)
    for direction in range(3):
        start = atom_count + 2 * direction * ghost_count
        from_lower = gradient[..., start:start + ghost_count]
        from_upper = gradient[..., start + ghost_count:start + 2 * ghost_count]
        back_upper = jnp.roll(from_lower, -1, axis=direction).reshape(-1, 3, ghost_count)
        back_lower = jnp.roll(from_upper, 1, axis=direction).reshape(-1, 3, ghost_count)
        flat_forces = add_cells(flat_forces, ghost_lists[:, :, :, direction, 0].reshape(-1, ghost_count), back_lower)
        flat_forces = add_cells(flat_forces, ghost_lists[:, :, :, direction, 1].reshape(-1, ghost_count), back_upper)
    forces = flat_forces.reshape(grid + (3, atom_count))

    def set_cols(target, chosen, values):
        return target.at[:, chosen].set(values)

    def set_rows(target, chosen, values):
        return target.at[chosen].set(values)
    set_pos = jax.vmap(set_cols)
    set_feat = jax.vmap(set_rows)
    move_count = move_lists.shape[5]
    moved_pos = places.reshape(-1, 3, atom_count)
    moved_feat = features.reshape(-1, atom_count, width)
    for direction in range(3):
        shift = (jnp.arange(3) == direction).astype(jnp.float32)[:, None] * cell_edge
        lower_slots = move_lists[:, :, :, direction, 0].reshape(-1, move_count)
        upper_slots = move_lists[:, :, :, direction, 1].reshape(-1, move_count)
        arrive_lower = jnp.roll(take_cols(places, move_lists[:, :, :, direction, 1]), 1, axis=direction) - shift
        arrive_upper = jnp.roll(take_cols(places, move_lists[:, :, :, direction, 0]), -1, axis=direction) + shift
        moved_pos = set_pos(moved_pos, lower_slots, arrive_lower.reshape(-1, 3, move_count))
        moved_pos = set_pos(moved_pos, upper_slots, arrive_upper.reshape(-1, 3, move_count))
        feat_lower = jnp.roll(take_rows(features, move_lists[:, :, :, direction, 1]), 1, axis=direction)
        feat_upper = jnp.roll(take_rows(features, move_lists[:, :, :, direction, 0]), -1, axis=direction)
        moved_feat = set_feat(moved_feat, lower_slots, feat_lower.reshape(-1, move_count, width))
        moved_feat = set_feat(moved_feat, upper_slots, feat_upper.reshape(-1, move_count, width))
    moved_positions = moved_pos.astype(jnp.bfloat16).reshape(positions.shape)
    moved_features = moved_feat.reshape(features.shape)
    return (forces, energy.reshape(grid + (atom_count,)), moved_positions, moved_features)
```

```python
import functools
import math

import jax
import jax.numpy as jnp
from jax import lax
from jax.experimental import pallas as pl
from jax.experimental.pallas import tpu as pltpu
from jax.sharding import PartitionSpec as P

cell_edge = 2.0
basis_width = 0.5
f32 = jnp.float32
bf16 = jnp.bfloat16
NT = (((1,), (1,)), ((), ()))
TN = (((0,), (0,)), ((), ()))
NN = (((1,), (0,)), ((), ()))


def dot(a, b, dims=NN):
    return lax.dot_general(a, b, dims, preferred_element_type=f32)


def slots_of(axes):
    slots = []
    for a, (_, size) in enumerate(axes):
        slots += [(a, (0, 1))] if size == 2 else [(a, (0,)), (a, (1,))]
    return slots


def sigmoid(x):
    return 0.5 * jnp.tanh(0.5 * x) + 0.5


def split(x):
    high = x.astype(bf16).astype(f32)
    return high, x - high


def kernel(
    axes,
    pos_ref,
    feat_ref,
    gl_ref,
    ml_ref,
    nb_ref,
    w_rad_ref,
    w_env_ref,
    w_scal_ref,
    w_out_ref,
    w_self_hbm,
    w_pair_hbm,
    w_mix_hbm,
    w_upd_hbm,
    force_ref,
    energy_ref,
    mpos_ref,
    mfeat_ref,
    w_self_ref,
    w_pair_ref,
    w_mix_ref,
    w_upd_ref,
    small_tx,
    small_rx,
    feats,
    grad_tx,
    grad_rx,
    w_sem,
    small_send,
    small_recv,
    feat_send,
    feat_recv,
    grad_send,
    grad_recv,
):
    atoms = pos_ref.shape[1]
    ghosts = gl_ref.shape[2]
    moves = ml_ref.shape[2]
    neigh = nb_ref.shape[0]
    edges = neigh * atoms
    ext = atoms + 6 * ghosts
    radial = w_rad_ref.shape[0]
    channels = w_env_ref.shape[1]
    slots = slots_of(axes)
    rows = atoms * (len(slots) + 1)
    slot_of = {(a, side): s for s, (a, sides) in enumerate(slots) for side in sides}

    def device(a, step):
        name, size = axes[a]
        return {name: lax.rem(lax.axis_index(name) + (step % size), size)}

    weights = []
    for q, (src, dst) in enumerate(
        (
            (w_pair_hbm, w_pair_ref),
            (w_self_hbm, w_self_ref),
            (w_mix_hbm, w_mix_ref),
            (w_upd_hbm, w_upd_ref),
        )
    ):
        copy = pltpu.make_async_copy(src, dst, w_sem.at[q])
        copy.start()
        weights.append(copy)

    barrier = pltpu.get_barrier_semaphore()
    for a, sides in slots:
        step = 1 if sides[0] == 0 else -1
        pl.semaphore_signal(
            barrier, inc=1, device_id=device(a, step), device_id_type=pl.DeviceIdType.MESH
        )

    small_tx[...] = jnp.zeros_like(small_tx)
    small_tx[0:3, 0:atoms] = pos_ref[...].astype(f32)
    for a in range(3):
        small_tx[8 + 2 * a : 10 + 2 * a, 0:ghosts] = gl_ref[a].astype(f32)
        small_tx[16 + 2 * a : 18 + 2 * a, 0:moves] = ml_ref[a].astype(f32)

    pl.semaphore_wait(barrier, len(slots))

    small_copies, feat_copies = [], []
    for s, (a, sides) in enumerate(slots):
        copy = pltpu.make_async_remote_copy(
            src_ref=small_tx,
            dst_ref=small_rx.at[s],
            send_sem=small_send.at[s],
            recv_sem=small_recv.at[s],
            device_id=device(a, 1 if sides[0] == 0 else -1),
            device_id_type=pl.DeviceIdType.MESH,
        )
        copy.start()
        small_copies.append(copy)
    for s, (a, sides) in enumerate(slots):
        copy = pltpu.make_async_remote_copy(
            src_ref=feat_ref,
            dst_ref=feats.at[pl.ds(atoms * (s + 1), atoms)],
            send_sem=feat_send.at[s],
            recv_sem=feat_recv.at[s],
            device_id=device(a, 1 if sides[0] == 0 else -1),
            device_id_type=pl.DeviceIdType.MESH,
        )
        copy.start()
        feat_copies.append(copy)

    own = feat_ref[...]
    feats[0:atoms, :] = own

    nb = nb_ref[...]
    nb_row = jnp.concatenate([nb[k : k + 1, :] for k in range(neigh)], axis=1)
    hot_ext = jnp.where(
        lax.broadcasted_iota(jnp.int32, (ext, edges), 0) == nb_row, 1.0, 0.0
    ).astype(bf16)
    places = small_tx[0:3, 0:atoms]

    def tile_atoms(x):
        return jnp.concatenate([x] * neigh, axis=1)

    centre = tile_atoms(places)
    shifts = []
    for a in range(3):
        start = atoms + 2 * a * ghosts
        lower = (nb_row >= start) & (nb_row < start + ghosts)
        upper = (nb_row >= start + ghosts) & (nb_row < start + 2 * ghosts)
        shifts.append(jnp.where(lower, -cell_edge, jnp.where(upper, cell_edge, 0.0)))
    w_env_t = jnp.transpose(w_env_ref[...].astype(f32)).astype(bf16)
    out_id = lax.broadcasted_iota(jnp.int32, (3 * channels, 3 * channels), 0)
    in_id = lax.broadcasted_iota(jnp.int32, (3 * channels, 3 * channels), 1)
    permute = jnp.where(
        in_id == (out_id % channels) * 3 + out_id // channels, 1.0, 0.0
    ).astype(bf16)
    w_scal = dot(permute, w_scal_ref[...].astype(bf16)).astype(bf16)
    w_rad_high, w_rad_low = split(w_rad_ref[...])
    w_out = w_out_ref[...]

    weights[1].wait()
    self_proj = dot(own, w_self_ref[...]).astype(bf16).astype(f32)

    for copy in small_copies:
        copy.wait_recv()
    pieces = [lax.broadcasted_iota(jnp.int32, (1, atoms), 1)]
    for q in range(6):
        a, side = q // 2, q % 2
        s = slot_of[(a, side)]
        row = 8 + 2 * a + 1 - side
        listed = small_rx[s, row : row + 1, 0:ghosts].astype(jnp.int32)
        pieces.append(listed + atoms * (s + 1))
    owner_row = jnp.concatenate(pieces, axis=1)
    hot_owner = jnp.where(
        lax.broadcasted_iota(jnp.int32, (rows, ext), 0) == owner_row, 1.0, 0.0
    ).astype(bf16)
    hot_t_wide = dot(hot_owner, hot_ext)
    hot_t = hot_t_wide.astype(bf16)
    hot = jnp.transpose(hot_t_wide).astype(bf16)
    places_all = jnp.concatenate(
        [small_tx[0:8, 0:atoms]] + [small_rx[s, 0:8, 0:atoms] for s in range(len(slots))], axis=1
    ).astype(bf16)
    partner = dot(places_all, hot_t)
    offset = [partner[a : a + 1, :] + shifts[a] - centre[a : a + 1, :] for a in range(3)]
    dist = jnp.sqrt(offset[0] * offset[0] + offset[1] * offset[1] + offset[2] * offset[2] + 0.25)
    inverse = 1.0 / dist
    ux, uy, uz = [o * inverse for o in offset]
    root3 = math.sqrt(3.0)
    root15 = math.sqrt(15.0)
    root5 = math.sqrt(5.0)
    harm = [
        None,
        root3 * ux,
        root3 * uy,
        root3 * uz,
        root15 * ux * uy,
        root15 * uy * uz,
        0.5 * root5 * (3.0 * uz * uz - 1.0),
        root15 * ux * uz,
        0.5 * root15 * (ux * ux - uy * uy),
    ]
    degree = [0, 1, 1, 1, 2, 2, 2, 2, 2]
    centres = basis_width * lax.broadcasted_iota(jnp.int32, (radial, edges), 0).astype(f32)
    away = dist - centres
    basis = jnp.exp(-jnp.square(away * (1.0 / basis_width)))
    basis_high, basis_low = split(basis)
    basis_cat = jnp.concatenate([basis_high, basis_low, basis_high], axis=0).astype(bf16)
    w_rad_cat = jnp.concatenate([w_rad_high, w_rad_high, w_rad_low], axis=0).astype(bf16)
    before = dot(basis_cat, w_rad_cat, TN) + jnp.concatenate([self_proj] * neigh, axis=0)

    weights[0].wait()
    for copy in feat_copies:
        copy.wait_recv()
    pair = dot(feats[...], w_pair_ref[...]).astype(bf16)
    before = before + dot(hot, pair)

    def silu_pair(x):
        gate = sigmoid(x)
        value = x * gate
        return value, gate + value * (1.0 - gate)

    latent, slope_a = silu_pair(before)
    weights[2].wait()
    mixed, slope_z = silu_pair(dot(latent.astype(bf16), w_mix_ref[...]))
    mixed = mixed.astype(bf16)
    env_w = dot(w_env_t, mixed, NT)

    def over_neighbours(x):
        total = x[:, 0:128]
        for q in range(1, edges // 128):
            total = total + x[:, 128 * q : 128 * (q + 1)]
        total = total + pltpu.roll(total, 64, 1)
        return jnp.concatenate([total] * (edges // 128), axis=1)

    scale = 1.0 / math.sqrt(neigh)

    def times(x, m):
        return x if harm[m] is None else x * harm[m]

    environment = [over_neighbours(times(env_w, m)) * scale for m in range(9)]
    invariants = [None, None, None]
    for m in range(9):
        term = times(environment[m], m)
        level = degree[m]
        invariants[level] = term if invariants[level] is None else invariants[level] + term
    invariants = jnp.concatenate(invariants, axis=0).astype(bf16)
    weights[3].wait()
    update, slope_y = silu_pair(dot(mixed, w_upd_ref[...]) + dot(invariants, w_scal, TN))
    total = update[0:atoms, :]
    for k in range(1, neigh):
        total = total + update[atoms * k : atoms * (k + 1), :]
    energy_ref[...] = lax.dot_general(
        w_out, total, NT, precision=lax.Precision.HIGHEST, preferred_element_type=f32
    )

    d_y = (slope_y * w_out).astype(bf16)
    d_inv = dot(w_scal, d_y, NT)
    d_harm = [None] * 9
    d_env_w = None
    for m in range(9):
        d_level = d_inv[channels * degree[m] : channels * (degree[m] + 1), :]
        d_environment = over_neighbours(times(d_level, m)) * scale
        back = times(d_environment, m)
        d_env_w = back if d_env_w is None else d_env_w + back
        if m:
            d_harm[m] = jnp.sum(
                d_level * environment[m] + d_environment * env_w, axis=0, keepdims=True
            )
    d_mixed = dot(d_y, w_upd_ref[...], NT) + dot(d_env_w.astype(bf16), w_env_t, TN)
    d_z = (slope_z * d_mixed).astype(bf16)
    d_before = (slope_a * dot(d_z, w_mix_ref[...], NT)).astype(bf16)
    w_rad_two = jnp.concatenate([w_rad_high, w_rad_low], axis=0).astype(bf16)
    d_basis = dot(w_rad_two, d_before, NT)
    d_basis = d_basis[0:radial, :] + d_basis[radial : 2 * radial, :]
    d_dist = jnp.sum(
        d_basis * basis * away * (-2.0 / basis_width**2), axis=0, keepdims=True
    )
    d_ux = root3 * d_harm[1] + root15 * (uy * d_harm[4] + uz * d_harm[7] + ux * d_harm[8])
    d_uy = root3 * d_harm[2] + root15 * (ux * d_harm[4] + uz * d_harm[5] - uy * d_harm[8])
    d_uz = (
        root3 * d_harm[3]
        + root15 * (uy * d_harm[5] + ux * d_harm[7])
        + (3.0 * root5) * uz * d_harm[6]
    )
    along = d_dist - (d_ux * ux + d_uy * uy + d_uz * uz) * inverse
    d_offset = jnp.concatenate(
        [
            d_ux * inverse + ux * along,
            d_uy * inverse + uy * along,
            d_uz * inverse + uz * along,
            jnp.zeros((5, edges), f32),
        ],
        axis=0,
    )
    d_high, d_low = split(d_offset)
    scattered = dot(jnp.concatenate([d_high, d_low], axis=0).astype(bf16), hot_t, NT)
    scattered = scattered[0:8, :] + scattered[8:16, :]
    for s in range(len(slots)):
        grad_tx[s, :, 0:atoms] = scattered[:, atoms * (s + 1) : atoms * (s + 2)]
    grad_copies = []
    for s, (a, sides) in enumerate(slots):
        copy = pltpu.make_async_remote_copy(
            src_ref=grad_tx.at[s],
            dst_ref=grad_rx.at[s],
            send_sem=grad_send.at[s],
            recv_sem=grad_recv.at[s],
            device_id=device(a, -1 if sides[0] == 0 else 1),
            device_id_type=pl.DeviceIdType.MESH,
        )
        copy.start()
        grad_copies.append(copy)
    gradient = scattered[:, 0:atoms] - over_neighbours(d_offset)[:, 0:atoms]

    slot_row = jnp.concatenate(
        [small_tx[16 + q : 17 + q, 0:moves] for q in range(6)], axis=1
    ).astype(jnp.int32)
    from_row = jnp.concatenate(
        [
            small_rx[slot_of[(q // 2, q % 2)], 16 + (q ^ 1) : 17 + (q ^ 1), 0:moves].astype(
                jnp.int32
            )
            + atoms * (slot_of[(q // 2, q % 2)] + 1)
            for q in range(6)
        ],
        axis=1,
    )
    slot_hot = jnp.where(
        lax.broadcasted_iota(jnp.int32, (atoms, 6 * moves), 0) == slot_row, 1.0, 0.0
    )
    from_hot = jnp.where(
        lax.broadcasted_iota(jnp.int32, (rows, 6 * moves), 0) == from_row, 1.0, 0.0
    ).astype(bf16)
    keeps = 1.0 - jnp.sum(slot_hot, axis=1, keepdims=True)
    same = lax.broadcasted_iota(jnp.int32, (atoms, rows), 0) == lax.broadcasted_iota(
        jnp.int32, (atoms, rows), 1
    )
    slot_hot = slot_hot.astype(bf16)
    source = (dot(slot_hot, from_hot, NT) + jnp.where(same, keeps, 0.0)).astype(bf16)
    mfeat_ref[...] = dot(source, feats[...]).astype(bf16)
    entry = lax.broadcasted_iota(jnp.int32, (8, 6 * moves), 1) // moves
    along_row = lax.broadcasted_iota(jnp.int32, (8, 6 * moves), 0)
    move_shift = jnp.where(
        entry == 2 * along_row, -cell_edge, jnp.where(entry == 2 * along_row + 1, cell_edge, 0.0)
    ).astype(bf16)
    moved = dot(places_all, source, NT) + dot(move_shift, slot_hot, NT)
    mpos_ref[...] = moved[0:3, :].astype(bf16)

    for s, copy in enumerate(grad_copies):
        copy.wait_recv()
        gradient = gradient + grad_rx[s, :, 0:atoms]
    force_ref[...] = -gradient[0:3, :]
    for copy in small_copies + feat_copies + grad_copies:
        copy.wait_send()


def shards(axes, *args):
    (
        positions,
        features,
        ghost_lists,
        move_lists,
        neighbours,
        w_self,
        w_pair,
        w_radial,
        w_mix,
        w_env,
        w_scal,
        w_upd,
        w_out,
    ) = args
    atoms = positions.shape[-1]
    width = features.shape[-1]
    count = len(slots_of(axes))
    in_vmem = pl.BlockSpec(memory_space=pltpu.VMEM)
    anywhere = pl.BlockSpec(memory_space=pl.ANY)
    semaphores = pltpu.SemaphoreType.DMA((count,))
    forces, energy, moved_positions, moved_features = pl.pallas_call(
        functools.partial(kernel, axes),
        out_shape=(
            jax.ShapeDtypeStruct((3, atoms), f32),
            jax.ShapeDtypeStruct((1, atoms), f32),
            jax.ShapeDtypeStruct((3, atoms), bf16),
            jax.ShapeDtypeStruct((atoms, width), bf16),
        ),
        in_specs=[in_vmem] * 9 + [anywhere] * 4,
        out_specs=(in_vmem,) * 4,
        scratch_shapes=[pltpu.VMEM((width, width), bf16)] * 4
        + [
            pltpu.VMEM((24, 128), f32),
            pltpu.VMEM((count, 24, 128), f32),
            pltpu.VMEM((atoms * (count + 1), width), bf16),
            pltpu.VMEM((count, 8, 128), f32),
            pltpu.VMEM((count, 8, 128), f32),
            pltpu.SemaphoreType.DMA((4,)),
        ]
        + [semaphores] * 6,
        compiler_params=pltpu.CompilerParams(
            collective_id=0, has_side_effects=True, vmem_limit_bytes=40 * 1024 * 1024
        ),
    )(
        positions.reshape(positions.shape[3:]),
        features.reshape(features.shape[3:]),
        ghost_lists.reshape(ghost_lists.shape[3:]),
        move_lists.reshape(move_lists.shape[3:]),
        neighbours.reshape(neighbours.shape[3:]),
        w_radial,
        w_env,
        w_scal,
        w_out.reshape(1, -1),
        w_self,
        w_pair,
        w_mix,
        w_upd,
    )
    return (
        forces.reshape(positions.shape),
        energy.reshape(1, 1, 1, atoms),
        moved_positions.reshape(positions.shape),
        moved_features.reshape(features.shape),
    )


def solution(mesh):
    axes = tuple((name, mesh.shape[name]) for name in ("gx", "gy", "gz"))
    cell = P("gx", "gy", "gz", None, None)
    lists = P("gx", "gy", "gz", None, None, None)
    return jax.shard_map(
        functools.partial(shards, axes),
        mesh=mesh,
        in_specs=(cell, cell, lists, lists, cell) + (P(),) * 8,
        out_specs=(cell, P("gx", "gy", "gz", None), cell, cell),
        check_vma=False,
    )
```

```python
import functools
import math

import jax
import jax.numpy as jnp
from jax import lax
from jax.experimental import pallas as pl
from jax.experimental.pallas import tpu as pltpu
from jax.sharding import PartitionSpec as P

VMEM_BYTES = 63 * 1024 * 1024 + 768 * 1024
cell_edge = 2.0
basis_width = 0.5
f32 = jnp.float32
bf16 = jnp.bfloat16
NT = (((1,), (1,)), ((), ()))
TN = (((0,), (0,)), ((), ()))
NN = (((1,), (0,)), ((), ()))


def dot(a, b, dims=NN):
    return lax.dot_general(a, b, dims, preferred_element_type=f32)


def slots_of(axes):
    slots = []
    for a, (_, size) in enumerate(axes):
        slots += [(a, (0, 1))] if size == 2 else [(a, (0,)), (a, (1,))]
    return slots


def sigmoid(x):
    return 0.5 * jnp.tanh(0.5 * x) + 0.5


def split(x):
    high = x.astype(bf16).astype(f32)
    return high, x - high


def kernel(
    axes,
    pos_hbm,
    feat_hbm,
    gl_hbm,
    ml_hbm,
    nb_hbm,
    w_rad_hbm,
    w_env_hbm,
    w_scal_hbm,
    w_out_hbm,
    w_self_hbm,
    w_pair_hbm,
    w_mix_hbm,
    w_upd_hbm,
    force_hbm,
    energy_hbm,
    mpos_hbm,
    mfeat_hbm,
    pos_ref,
    gl_ref,
    ml_ref,
    nb_ref,
    w_rad_ref,
    w_env_ref,
    w_scal_ref,
    w_out_ref,
    w_self_ref,
    w_pair_ref,
    w_mix_ref,
    w_upd_ref,
    small_tx,
    small_rx,
    feats,
    grad_tx,
    grad_rx,
    force_ref,
    energy_ref,
    mpos_ref,
    mfeat_ref,
    load_sem,
    store_sem,
    small_send,
    small_recv,
    feat_send,
    feat_recv,
    grad_send,
    grad_recv,
):
    atoms = pos_ref.shape[1]
    ghosts = gl_ref.shape[2]
    moves = ml_ref.shape[2]
    neigh = nb_ref.shape[0]
    edges = neigh * atoms
    ext = atoms + 6 * ghosts
    radial = w_rad_ref.shape[0]
    channels = w_env_ref.shape[0]
    slots = slots_of(axes)
    rows = atoms * (len(slots) + 1)
    slot_of = {(a, side): s for s, (a, sides) in enumerate(slots) for side in sides}

    def device(a, step):
        name, size = axes[a]
        return {name: lax.rem(lax.axis_index(name) + (step % size), size)}

    barrier = pltpu.get_barrier_semaphore()
    for a, sides in slots:
        step = 1 if sides[0] == 0 else -1
        pl.semaphore_signal(
            barrier, inc=1, device_id=device(a, step), device_id_type=pl.DeviceIdType.MESH
        )

    loads = {}
    for q, (name, src, dst) in enumerate(
        (
            ("pos", pos_hbm, pos_ref),
            ("gl", gl_hbm, gl_ref),
            ("ml", ml_hbm, ml_ref),
            ("nb", nb_hbm, nb_ref),
            ("feat", feat_hbm, feats.at[pl.ds(0, atoms)]),
            ("self", w_self_hbm, w_self_ref),
            ("scal", w_scal_hbm, w_scal_ref),
            ("rad", w_rad_hbm, w_rad_ref),
            ("env", w_env_hbm, w_env_ref),
            ("out", w_out_hbm, w_out_ref),
            ("pair", w_pair_hbm, w_pair_ref),
            ("mix", w_mix_hbm, w_mix_ref),
            ("upd", w_upd_hbm, w_upd_ref),
        )
    ):
        loads[name] = pltpu.make_async_copy(src, dst, load_sem.at[q])
        loads[name].start()

    small_tx[...] = jnp.zeros_like(small_tx)
    for name in ("pos", "gl", "ml"):
        loads[name].wait()
    small_tx[0:3, 0:atoms] = pos_ref[...].astype(f32)
    for a in range(3):
        small_tx[8 + 2 * a : 10 + 2 * a, 0:ghosts] = gl_ref[a].astype(f32)
        small_tx[16 + 2 * a : 18 + 2 * a, 0:moves] = ml_ref[a].astype(f32)

    pl.semaphore_wait(barrier, len(slots))

    small_copies, feat_copies = [], []
    for s, (a, sides) in enumerate(slots):
        copy = pltpu.make_async_remote_copy(
            src_ref=small_tx,
            dst_ref=small_rx.at[s],
            send_sem=small_send.at[s],
            recv_sem=small_recv.at[s],
            device_id=device(a, 1 if sides[0] == 0 else -1),
            device_id_type=pl.DeviceIdType.MESH,
        )
        copy.start()
        small_copies.append(copy)
    for s, (a, sides) in enumerate(slots):
        copy = pltpu.make_async_remote_copy(
            src_ref=feat_hbm,
            dst_ref=feats.at[pl.ds(atoms * (s + 1), atoms)],
            send_sem=feat_send.at[s],
            recv_sem=feat_recv.at[s],
            device_id=device(a, 1 if sides[0] == 0 else -1),
            device_id_type=pl.DeviceIdType.MESH,
        )
        copy.start()
        feat_copies.append(copy)

    loads["nb"].wait()
    nb = nb_ref[...]
    nb_row = jnp.concatenate([nb[k : k + 1, :] for k in range(neigh)], axis=1)
    hot_ext = jnp.where(
        lax.broadcasted_iota(jnp.int32, (ext, edges), 0) == nb_row, 1.0, 0.0
    ).astype(bf16)
    places = small_tx[0:3, 0:atoms]

    def tile_atoms(x):
        return jnp.concatenate([x] * neigh, axis=1)

    centre = tile_atoms(places)
    shifts = []
    for a in range(3):
        start = atoms + 2 * a * ghosts
        lower = (nb_row >= start) & (nb_row < start + ghosts)
        upper = (nb_row >= start + ghosts) & (nb_row < start + 2 * ghosts)
        shifts.append(jnp.where(lower, -cell_edge, jnp.where(upper, cell_edge, 0.0)))
    for name in ("scal", "rad", "env", "out", "feat", "self"):
        loads[name].wait()
    w_env_t = w_env_ref[...]
    out_id = lax.broadcasted_iota(jnp.int32, (3 * channels, 3 * channels), 0)
    in_id = lax.broadcasted_iota(jnp.int32, (3 * channels, 3 * channels), 1)
    permute = jnp.where(
        in_id == (out_id % channels) * 3 + out_id // channels, 1.0, 0.0
    ).astype(bf16)
    w_scal = dot(permute, w_scal_ref[...].astype(bf16)).astype(bf16)
    w_rad_high, w_rad_low = split(w_rad_ref[...])
    w_out = w_out_ref[...]

    self_proj = dot(feats[0:atoms, :], w_self_ref[...]).astype(bf16).astype(f32)

    for copy in small_copies:
        copy.wait_recv()
    pieces = [lax.broadcasted_iota(jnp.int32, (1, atoms), 1)]
    for q in range(6):
        a, side = q // 2, q % 2
        s = slot_of[(a, side)]
        row = 8 + 2 * a + 1 - side
        listed = small_rx[s, row : row + 1, 0:ghosts].astype(jnp.int32)
        pieces.append(listed + atoms * (s + 1))
    owner_row = jnp.concatenate(pieces, axis=1)
    hot_owner = jnp.where(
        lax.broadcasted_iota(jnp.int32, (rows, ext), 0) == owner_row, 1.0, 0.0
    ).astype(bf16)
    hot_t_wide = dot(hot_owner, hot_ext)
    hot_t = hot_t_wide.astype(bf16)
    hot = jnp.transpose(hot_t_wide).astype(bf16)
    places_all = jnp.concatenate(
        [small_tx[0:8, 0:atoms]] + [small_rx[s, 0:8, 0:atoms] for s in range(len(slots))], axis=1
    ).astype(bf16)
    partner = dot(places_all, hot_t)
    offset = [partner[a : a + 1, :] + shifts[a] - centre[a : a + 1, :] for a in range(3)]
    dist = jnp.sqrt(offset[0] * offset[0] + offset[1] * offset[1] + offset[2] * offset[2] + 0.25)
    inverse = 1.0 / dist
    ux, uy, uz = [o * inverse for o in offset]
    root3 = math.sqrt(3.0)
    root15 = math.sqrt(15.0)
    root5 = math.sqrt(5.0)
    harm = [
        None,
        root3 * ux,
        root3 * uy,
        root3 * uz,
        root15 * ux * uy,
        root15 * uy * uz,
        0.5 * root5 * (3.0 * uz * uz - 1.0),
        root15 * ux * uz,
        0.5 * root15 * (ux * ux - uy * uy),
    ]
    degree = [0, 1, 1, 1, 2, 2, 2, 2, 2]
    centres = basis_width * lax.broadcasted_iota(jnp.int32, (radial, edges), 0).astype(f32)
    away = dist - centres
    basis = jnp.exp(-jnp.square(away * (1.0 / basis_width)))
    basis_high, basis_low = split(basis)
    basis_cat = jnp.concatenate([basis_high, basis_low, basis_high], axis=0).astype(bf16)
    w_rad_cat = jnp.concatenate([w_rad_high, w_rad_high, w_rad_low], axis=0).astype(bf16)
    before = dot(basis_cat, w_rad_cat, TN) + jnp.concatenate([self_proj] * neigh, axis=0)

    loads["pair"].wait()
    for copy in feat_copies:
        copy.wait_recv()
    pair = dot(feats[...], w_pair_ref[...]).astype(bf16)
    before = before + dot(hot, pair)

    def silu_pair(x):
        gate = sigmoid(x)
        value = x * gate
        return value, gate + value * (1.0 - gate)

    latent, slope_a = silu_pair(before)
    loads["mix"].wait()
    mixed, slope_z = silu_pair(dot(latent.astype(bf16), w_mix_ref[...]))
    mixed = mixed.astype(bf16)
    env_w = dot(w_env_t, mixed, NT)

    def over_neighbours(x):
        total = x[:, 0:128]
        for q in range(1, edges // 128):
            total = total + x[:, 128 * q : 128 * (q + 1)]
        total = total + pltpu.roll(total, 64, 1)
        return jnp.concatenate([total] * (edges // 128), axis=1)

    scale = 1.0 / math.sqrt(neigh)

    def times(x, m):
        return x if harm[m] is None else x * harm[m]

    environment = [over_neighbours(times(env_w, m)) * scale for m in range(9)]
    invariants = [None, None, None]
    for m in range(9):
        term = times(environment[m], m)
        level = degree[m]
        invariants[level] = term if invariants[level] is None else invariants[level] + term
    invariants = jnp.concatenate(invariants, axis=0).astype(bf16)
    loads["upd"].wait()
    update, slope_y = silu_pair(dot(mixed, w_upd_ref[...]) + dot(invariants, w_scal, TN))
    total = update[0:atoms, :]
    for k in range(1, neigh):
        total = total + update[atoms * k : atoms * (k + 1), :]
    energy_ref[...] = lax.dot_general(
        w_out, total, NT, precision=lax.Precision.HIGHEST, preferred_element_type=f32
    )

    energy_copy = pltpu.make_async_copy(energy_ref, energy_hbm, store_sem.at[0])
    energy_copy.start()

    d_y = (slope_y * w_out).astype(bf16)
    d_inv = dot(w_scal, d_y, NT)
    d_harm = [None] * 9
    d_env_w = None
    for m in range(9):
        d_level = d_inv[channels * degree[m] : channels * (degree[m] + 1), :]
        d_environment = over_neighbours(times(d_level, m)) * scale
        back = times(d_environment, m)
        d_env_w = back if d_env_w is None else d_env_w + back
        if m:
            d_harm[m] = jnp.sum(
                d_level * environment[m] + d_environment * env_w, axis=0, keepdims=True
            )
    d_mixed = dot(d_y, w_upd_ref[...], NT) + dot(d_env_w.astype(bf16), w_env_t, TN)
    d_z = (slope_z * d_mixed).astype(bf16)
    d_before = (slope_a * dot(d_z, w_mix_ref[...], NT)).astype(bf16)
    w_rad_two = jnp.concatenate([w_rad_high, w_rad_low], axis=0).astype(bf16)
    d_basis = dot(w_rad_two, d_before, NT)
    d_basis = d_basis[0:radial, :] + d_basis[radial : 2 * radial, :]
    d_dist = jnp.sum(
        d_basis * basis * away * (-2.0 / basis_width**2), axis=0, keepdims=True
    )
    d_ux = root3 * d_harm[1] + root15 * (uy * d_harm[4] + uz * d_harm[7] + ux * d_harm[8])
    d_uy = root3 * d_harm[2] + root15 * (ux * d_harm[4] + uz * d_harm[5] - uy * d_harm[8])
    d_uz = (
        root3 * d_harm[3]
        + root15 * (uy * d_harm[5] + ux * d_harm[7])
        + (3.0 * root5) * uz * d_harm[6]
    )
    along = d_dist - (d_ux * ux + d_uy * uy + d_uz * uz) * inverse
    d_offset = jnp.concatenate(
        [
            d_ux * inverse + ux * along,
            d_uy * inverse + uy * along,
            d_uz * inverse + uz * along,
            jnp.zeros((5, edges), f32),
        ],
        axis=0,
    )
    d_high, d_low = split(d_offset)
    scattered = dot(jnp.concatenate([d_high, d_low], axis=0).astype(bf16), hot_t, NT)
    scattered = scattered[0:8, :] + scattered[8:16, :]
    for s in range(len(slots)):
        grad_tx[s, :, 0:atoms] = scattered[:, atoms * (s + 1) : atoms * (s + 2)]
    grad_copies = []
    for s, (a, sides) in enumerate(slots):
        copy = pltpu.make_async_remote_copy(
            src_ref=grad_tx.at[s],
            dst_ref=grad_rx.at[s],
            send_sem=grad_send.at[s],
            recv_sem=grad_recv.at[s],
            device_id=device(a, -1 if sides[0] == 0 else 1),
            device_id_type=pl.DeviceIdType.MESH,
        )
        copy.start()
        grad_copies.append(copy)
    gradient = scattered[:, 0:atoms] - over_neighbours(d_offset)[:, 0:atoms]

    slot_row = jnp.concatenate(
        [small_tx[16 + q : 17 + q, 0:moves] for q in range(6)], axis=1
    ).astype(jnp.int32)
    from_row = jnp.concatenate(
        [
            small_rx[slot_of[(q // 2, q % 2)], 16 + (q ^ 1) : 17 + (q ^ 1), 0:moves].astype(
                jnp.int32
            )
            + atoms * (slot_of[(q // 2, q % 2)] + 1)
            for q in range(6)
        ],
        axis=1,
    )
    slot_hot = jnp.where(
        lax.broadcasted_iota(jnp.int32, (atoms, 6 * moves), 0) == slot_row, 1.0, 0.0
    )
    from_hot = jnp.where(
        lax.broadcasted_iota(jnp.int32, (rows, 6 * moves), 0) == from_row, 1.0, 0.0
    ).astype(bf16)
    keeps = 1.0 - jnp.sum(slot_hot, axis=1, keepdims=True)
    same = lax.broadcasted_iota(jnp.int32, (atoms, rows), 0) == lax.broadcasted_iota(
        jnp.int32, (atoms, rows), 1
    )
    slot_hot = slot_hot.astype(bf16)
    source = (dot(slot_hot, from_hot, NT) + jnp.where(same, keeps, 0.0)).astype(bf16)
    mfeat_ref[...] = dot(source, feats[...]).astype(bf16)
    entry = lax.broadcasted_iota(jnp.int32, (8, 6 * moves), 1) // moves
    along_row = lax.broadcasted_iota(jnp.int32, (8, 6 * moves), 0)
    move_shift = jnp.where(
        entry == 2 * along_row, -cell_edge, jnp.where(entry == 2 * along_row + 1, cell_edge, 0.0)
    ).astype(bf16)
    moved = dot(places_all, source, NT) + dot(move_shift, slot_hot, NT)
    mpos_ref[...] = moved[0:3, :].astype(bf16)
    mfeat_copy = pltpu.make_async_copy(mfeat_ref, mfeat_hbm, store_sem.at[1])
    mfeat_copy.start()
    mpos_copy = pltpu.make_async_copy(mpos_ref, mpos_hbm, store_sem.at[2])
    mpos_copy.start()

    for s, copy in enumerate(grad_copies):
        copy.wait_recv()
        gradient = gradient + grad_rx[s, :, 0:atoms]
    for a in range(3):
        force_ref[a] = -gradient[a : a + 1, :]
    force_copy = pltpu.make_async_copy(force_ref, force_hbm, store_sem.at[3])
    force_copy.start()
    for copy in small_copies + feat_copies + grad_copies:
        copy.wait_send()
    for copy in (energy_copy, mfeat_copy, mpos_copy, force_copy):
        copy.wait()


def finish(*refs):
    count = len(refs) // 2
    copies = [
        pltpu.make_async_copy(refs[q], refs[count + q], refs[-1].at[q]) for q in range(count)
    ]
    for copy in copies:
        copy.start()
    for copy in copies:
        copy.wait()


def shards(axes, *args):
    (
        positions,
        features,
        ghost_lists,
        move_lists,
        neighbours,
        w_self,
        w_pair,
        w_radial,
        w_mix,
        w_env,
        w_scal,
        w_upd,
        w_out,
    ) = args
    atoms = positions.shape[-1]
    width = features.shape[-1]
    count = len(slots_of(axes))
    anywhere = pl.BlockSpec(memory_space=pl.ANY)
    semaphores = pltpu.SemaphoreType.DMA((count,))
    operands = (
        positions.reshape(positions.shape[3:]),
        features.reshape(features.shape[3:]),
        ghost_lists.reshape(ghost_lists.shape[3:]),
        move_lists.reshape(move_lists.shape[3:]),
        neighbours.reshape(neighbours.shape[3:]),
        w_radial,
        w_env.T,
        w_scal,
        w_out.reshape(1, -1),
        w_self,
        w_pair,
        w_mix,
        w_upd,
    )
    results = (
        jax.ShapeDtypeStruct((3, 1, atoms), f32),
        jax.ShapeDtypeStruct((1, atoms), f32),
        jax.ShapeDtypeStruct((3, atoms), bf16),
        jax.ShapeDtypeStruct((atoms, width), bf16),
    )
    found = pl.pallas_call(
        functools.partial(kernel, axes),
        out_shape=results,
        in_specs=[anywhere] * len(operands),
        out_specs=(anywhere,) * 4,
        scratch_shapes=[
            pltpu.VMEM(operands[q].shape, operands[q].dtype)
            for q in (0, 2, 3, 4, 5, 6, 7, 8, 9, 10, 11, 12)
        ]
        + [
            pltpu.VMEM((24, 128), f32),
            pltpu.VMEM((count, 24, 128), f32),
            pltpu.VMEM((atoms * (count + 1), width), bf16),
            pltpu.VMEM((count, 8, 128), f32),
            pltpu.VMEM((count, 8, 128), f32),
        ]
        + [pltpu.VMEM(result.shape, result.dtype) for result in results]
        + [
            pltpu.SemaphoreType.DMA((len(operands),)),
            pltpu.SemaphoreType.DMA((4,)),
        ]
        + [semaphores] * 6,
        compiler_params=pltpu.CompilerParams(
            collective_id=0, has_side_effects=True, vmem_limit_bytes=VMEM_BYTES
        ),
    )(*operands)
    forces, energy, moved_positions, moved_features = pl.pallas_call(
        finish,
        out_shape=results,
        in_specs=[anywhere] * 4,
        out_specs=(anywhere,) * 4,
        scratch_shapes=[pltpu.SemaphoreType.DMA((4,))],
    )(*found)
    return (
        forces.reshape(positions.shape),
        energy.reshape(1, 1, 1, atoms),
        moved_positions.reshape(positions.shape),
        moved_features.reshape(features.shape),
    )


def solution(mesh):
    axes = tuple((name, mesh.shape[name]) for name in ("gx", "gy", "gz"))
    cell = P("gx", "gy", "gz", None, None)
    lists = P("gx", "gy", "gz", None, None, None)
    return jax.shard_map(
        functools.partial(shards, axes),
        mesh=mesh,
        in_specs=(cell, cell, lists, lists, cell) + (P(),) * 8,
        out_specs=(cell, P("gx", "gy", "gz", None), cell, cell),
        check_vma=False,
    )
```

```python
import functools
import math

import jax
import jax.numpy as jnp
from jax import lax
from jax.experimental import pallas as pl
from jax.experimental.pallas import tpu as pltpu
from jax.sharding import PartitionSpec as P

VMEM_BYTES = 63 * 1024 * 1024 + 768 * 1024
cell_edge = 2.0
basis_width = 0.5
f32 = jnp.float32
bf16 = jnp.bfloat16
NT = (((1,), (1,)), ((), ()))
TN = (((0,), (0,)), ((), ()))
NN = (((1,), (0,)), ((), ()))


def dot(a, b, dims=NN):
    return lax.dot_general(a, b, dims, preferred_element_type=f32)


def slots_of(axes):
    slots = []
    for a, (_, size) in enumerate(axes):
        slots += [(a, (0, 1))] if size == 2 else [(a, (0,)), (a, (1,))]
    return slots


def sigmoid(x):
    return 0.5 * jnp.tanh(0.5 * x) + 0.5


def split(x):
    high = x.astype(bf16).astype(f32)
    return high, x - high


def kernel(
    axes,
    pos_hbm,
    feat_hbm,
    gl_hbm,
    ml_hbm,
    nb_hbm,
    w_rad_hbm,
    w_env_hbm,
    w_scal_hbm,
    w_out_hbm,
    w_self_hbm,
    w_pair_hbm,
    w_mix_hbm,
    w_upd_hbm,
    force_hbm,
    energy_hbm,
    mpos_hbm,
    mfeat_hbm,
    pos_ref,
    gl_ref,
    ml_ref,
    nb_ref,
    w_rad_ref,
    w_env_ref,
    w_scal_ref,
    w_out_ref,
    w_self_ref,
    w_pair_ref,
    w_mix_ref,
    w_upd_ref,
    small_tx,
    small_rx,
    feats,
    grad_tx,
    grad_rx,
    force_ref,
    energy_ref,
    mpos_ref,
    mfeat_ref,
    load_sem,
    store_sem,
    small_send,
    small_recv,
    feat_send,
    feat_recv,
    grad_send,
    grad_recv,
):
    atoms = pos_ref.shape[1]
    ghosts = gl_ref.shape[2]
    moves = ml_ref.shape[2]
    neigh = nb_ref.shape[0]
    edges = neigh * atoms
    ext = atoms + 6 * ghosts
    radial = w_rad_ref.shape[0]
    channels = w_env_ref.shape[0]
    slots = slots_of(axes)
    rows = atoms * (len(slots) + 1)
    slot_of = {(a, side): s for s, (a, sides) in enumerate(slots) for side in sides}

    def device(a, step):
        name, size = axes[a]
        return {name: lax.rem(lax.axis_index(name) + (step % size), size)}

    barrier = pltpu.get_barrier_semaphore()
    for a, sides in slots:
        step = 1 if sides[0] == 0 else -1
        pl.semaphore_signal(
            barrier, inc=1, device_id=device(a, step), device_id_type=pl.DeviceIdType.MESH
        )

    loads = {}
    for q, (name, src, dst) in enumerate(
        (
            ("pos", pos_hbm, pos_ref),
            ("gl", gl_hbm, gl_ref),
            ("ml", ml_hbm, ml_ref),
            ("nb", nb_hbm, nb_ref),
            ("feat", feat_hbm, feats.at[pl.ds(0, atoms)]),
            ("self", w_self_hbm, w_self_ref),
            ("scal", w_scal_hbm, w_scal_ref),
            ("rad", w_rad_hbm, w_rad_ref),
            ("env", w_env_hbm, w_env_ref),
            ("out", w_out_hbm, w_out_ref),
            ("pair", w_pair_hbm, w_pair_ref),
            ("mix", w_mix_hbm, w_mix_ref),
            ("upd", w_upd_hbm, w_upd_ref),
        )
    ):
        loads[name] = pltpu.make_async_copy(src, dst, load_sem.at[q])
    for name in ("pos", "gl", "ml", "nb"):
        loads[name].start()

    small_tx[...] = jnp.zeros_like(small_tx)
    for name in ("pos", "gl", "ml"):
        loads[name].wait()
    small_tx[0:3, 0:atoms] = pos_ref[...].astype(f32)
    for a in range(3):
        small_tx[8 + 2 * a : 10 + 2 * a, 0:ghosts] = gl_ref[a].astype(f32)
        small_tx[16 + 2 * a : 18 + 2 * a, 0:moves] = ml_ref[a].astype(f32)

    pl.semaphore_wait(barrier, len(slots))

    small_copies, feat_copies = [], []
    for s, (a, sides) in enumerate(slots):
        copy = pltpu.make_async_remote_copy(
            src_ref=small_tx,
            dst_ref=small_rx.at[s],
            send_sem=small_send.at[s],
            recv_sem=small_recv.at[s],
            device_id=device(a, 1 if sides[0] == 0 else -1),
            device_id_type=pl.DeviceIdType.MESH,
        )
        copy.start()
        small_copies.append(copy)
    for s, (a, sides) in enumerate(slots):
        copy = pltpu.make_async_remote_copy(
            src_ref=feat_hbm,
            dst_ref=feats.at[pl.ds(atoms * (s + 1), atoms)],
            send_sem=feat_send.at[s],
            recv_sem=feat_recv.at[s],
            device_id=device(a, 1 if sides[0] == 0 else -1),
            device_id_type=pl.DeviceIdType.MESH,
        )
        copy.start()
        feat_copies.append(copy)

    for name in list(loads)[4:]:
        loads[name].start()

    loads["nb"].wait()
    nb = nb_ref[...]
    nb_row = jnp.concatenate([nb[k : k + 1, :] for k in range(neigh)], axis=1)
    hot_ext = jnp.where(
        lax.broadcasted_iota(jnp.int32, (ext, edges), 0) == nb_row, 1.0, 0.0
    ).astype(bf16)
    places = small_tx[0:3, 0:atoms]

    def tile_atoms(x):
        return jnp.concatenate([x] * neigh, axis=1)

    centre = tile_atoms(places)
    shifts = []
    for a in range(3):
        start = atoms + 2 * a * ghosts
        lower = (nb_row >= start) & (nb_row < start + ghosts)
        upper = (nb_row >= start + ghosts) & (nb_row < start + 2 * ghosts)
        shifts.append(jnp.where(lower, -cell_edge, jnp.where(upper, cell_edge, 0.0)))
    for name in ("scal", "rad", "env", "out", "feat", "self"):
        loads[name].wait()
    w_env_t = w_env_ref[...]
    out_id = lax.broadcasted_iota(jnp.int32, (3 * channels, 3 * channels), 0)
    in_id = lax.broadcasted_iota(jnp.int32, (3 * channels, 3 * channels), 1)
    permute = jnp.where(
        in_id == (out_id % channels) * 3 + out_id // channels, 1.0, 0.0
    ).astype(bf16)
    w_scal = dot(permute, w_scal_ref[...].astype(bf16)).astype(bf16)
    w_rad_high, w_rad_low = split(w_rad_ref[...])
    w_out = w_out_ref[...]

    self_proj = dot(feats[0:atoms, :], w_self_ref[...]).astype(bf16).astype(f32)

    for copy in small_copies:
        copy.wait_recv()
    pieces = [lax.broadcasted_iota(jnp.int32, (1, atoms), 1)]
    for q in range(6):
        a, side = q // 2, q % 2
        s = slot_of[(a, side)]
        row = 8 + 2 * a + 1 - side
        listed = small_rx[s, row : row + 1, 0:ghosts].astype(jnp.int32)
        pieces.append(listed + atoms * (s + 1))
    owner_row = jnp.concatenate(pieces, axis=1)
    hot_owner = jnp.where(
        lax.broadcasted_iota(jnp.int32, (rows, ext), 0) == owner_row, 1.0, 0.0
    ).astype(bf16)
    hot_t_wide = dot(hot_owner, hot_ext)
    hot_t = hot_t_wide.astype(bf16)
    hot = jnp.transpose(hot_t_wide).astype(bf16)
    places_all = jnp.concatenate(
        [small_tx[0:8, 0:atoms]] + [small_rx[s, 0:8, 0:atoms] for s in range(len(slots))], axis=1
    ).astype(bf16)
    partner = dot(places_all, hot_t)
    offset = [partner[a : a + 1, :] + shifts[a] - centre[a : a + 1, :] for a in range(3)]
    dist = jnp.sqrt(offset[0] * offset[0] + offset[1] * offset[1] + offset[2] * offset[2] + 0.25)
    inverse = 1.0 / dist
    ux, uy, uz = [o * inverse for o in offset]
    root3 = math.sqrt(3.0)
    root15 = math.sqrt(15.0)
    root5 = math.sqrt(5.0)
    harm = [
        None,
        root3 * ux,
        root3 * uy,
        root3 * uz,
        root15 * ux * uy,
        root15 * uy * uz,
        0.5 * root5 * (3.0 * uz * uz - 1.0),
        root15 * ux * uz,
        0.5 * root15 * (ux * ux - uy * uy),
    ]
    degree = [0, 1, 1, 1, 2, 2, 2, 2, 2]
    centres = basis_width * lax.broadcasted_iota(jnp.int32, (radial, edges), 0).astype(f32)
    away = dist - centres
    basis = jnp.exp(-jnp.square(away * (1.0 / basis_width)))
    basis_high, basis_low = split(basis)
    basis_cat = jnp.concatenate([basis_high, basis_low, basis_high], axis=0).astype(bf16)
    w_rad_cat = jnp.concatenate([w_rad_high, w_rad_high, w_rad_low], axis=0).astype(bf16)
    before = dot(basis_cat, w_rad_cat, TN) + jnp.concatenate([self_proj] * neigh, axis=0)

    loads["pair"].wait()
    for copy in feat_copies:
        copy.wait_recv()
    pair = dot(feats[...], w_pair_ref[...]).astype(bf16)
    before = before + dot(hot, pair)

    def silu_pair(x):
        gate = sigmoid(x)
        value = x * gate
        return value, gate + value * (1.0 - gate)

    latent, slope_a = silu_pair(before)
    loads["mix"].wait()
    mixed, slope_z = silu_pair(dot(latent.astype(bf16), w_mix_ref[...]))
    mixed = mixed.astype(bf16)
    env_w = dot(w_env_t, mixed, NT)

    def over_neighbours(x):
        total = x[:, 0:128]
        for q in range(1, edges // 128):
            total = total + x[:, 128 * q : 128 * (q + 1)]
        total = total + pltpu.roll(total, 64, 1)
        return jnp.concatenate([total] * (edges // 128), axis=1)

    scale = 1.0 / math.sqrt(neigh)

    def times(x, m):
        return x if harm[m] is None else x * harm[m]

    environment = [over_neighbours(times(env_w, m)) * scale for m in range(9)]
    invariants = [None, None, None]
    for m in range(9):
        term = times(environment[m], m)
        level = degree[m]
        invariants[level] = term if invariants[level] is None else invariants[level] + term
    invariants = jnp.concatenate(invariants, axis=0).astype(bf16)
    loads["upd"].wait()
    update, slope_y = silu_pair(dot(mixed, w_upd_ref[...]) + dot(invariants, w_scal, TN))
    total = update[0:atoms, :]
    for k in range(1, neigh):
        total = total + update[atoms * k : atoms * (k + 1), :]
    energy_ref[...] = lax.dot_general(
        w_out, total, NT, precision=lax.Precision.HIGHEST, preferred_element_type=f32
    )

    energy_copy = pltpu.make_async_copy(energy_ref, energy_hbm, store_sem.at[0])
    energy_copy.start()

    d_y = (slope_y * w_out).astype(bf16)
    d_inv = dot(w_scal, d_y, NT)
    d_harm = [None] * 9
    d_env_w = None
    for m in range(9):
        d_level = d_inv[channels * degree[m] : channels * (degree[m] + 1), :]
        d_environment = over_neighbours(times(d_level, m)) * scale
        back = times(d_environment, m)
        d_env_w = back if d_env_w is None else d_env_w + back
        if m:
            d_harm[m] = jnp.sum(
                d_level * environment[m] + d_environment * env_w, axis=0, keepdims=True
            )
    d_mixed = dot(d_y, w_upd_ref[...], NT) + dot(d_env_w.astype(bf16), w_env_t, TN)
    d_z = (slope_z * d_mixed).astype(bf16)
    d_before = (slope_a * dot(d_z, w_mix_ref[...], NT)).astype(bf16)
    w_rad_two = jnp.concatenate([w_rad_high, w_rad_low], axis=0).astype(bf16)
    d_basis = dot(w_rad_two, d_before, NT)
    d_basis = d_basis[0:radial, :] + d_basis[radial : 2 * radial, :]
    d_dist = jnp.sum(
        d_basis * basis * away * (-2.0 / basis_width**2), axis=0, keepdims=True
    )
    d_ux = root3 * d_harm[1] + root15 * (uy * d_harm[4] + uz * d_harm[7] + ux * d_harm[8])
    d_uy = root3 * d_harm[2] + root15 * (ux * d_harm[4] + uz * d_harm[5] - uy * d_harm[8])
    d_uz = (
        root3 * d_harm[3]
        + root15 * (uy * d_harm[5] + ux * d_harm[7])
        + (3.0 * root5) * uz * d_harm[6]
    )
    along = d_dist - (d_ux * ux + d_uy * uy + d_uz * uz) * inverse
    d_offset = jnp.concatenate(
        [
            d_ux * inverse + ux * along,
            d_uy * inverse + uy * along,
            d_uz * inverse + uz * along,
            jnp.zeros((5, edges), f32),
        ],
        axis=0,
    )
    d_high, d_low = split(d_offset)
    scattered = dot(jnp.concatenate([d_high, d_low], axis=0).astype(bf16), hot_t, NT)
    scattered = scattered[0:8, :] + scattered[8:16, :]
    for s in range(len(slots)):
        grad_tx[s, :, 0:atoms] = scattered[:, atoms * (s + 1) : atoms * (s + 2)]
    grad_copies = []
    for s, (a, sides) in enumerate(slots):
        copy = pltpu.make_async_remote_copy(
            src_ref=grad_tx.at[s],
            dst_ref=grad_rx.at[s],
            send_sem=grad_send.at[s],
            recv_sem=grad_recv.at[s],
            device_id=device(a, -1 if sides[0] == 0 else 1),
            device_id_type=pl.DeviceIdType.MESH,
        )
        copy.start()
        grad_copies.append(copy)
    gradient = scattered[:, 0:atoms] - over_neighbours(d_offset)[:, 0:atoms]

    slot_row = jnp.concatenate(
        [small_tx[16 + q : 17 + q, 0:moves] for q in range(6)], axis=1
    ).astype(jnp.int32)
    from_row = jnp.concatenate(
        [
            small_rx[slot_of[(q // 2, q % 2)], 16 + (q ^ 1) : 17 + (q ^ 1), 0:moves].astype(
                jnp.int32
            )
            + atoms * (slot_of[(q // 2, q % 2)] + 1)
            for q in range(6)
        ],
        axis=1,
    )
    slot_hot = jnp.where(
        lax.broadcasted_iota(jnp.int32, (atoms, 6 * moves), 0) == slot_row, 1.0, 0.0
    )
    from_hot = jnp.where(
        lax.broadcasted_iota(jnp.int32, (rows, 6 * moves), 0) == from_row, 1.0, 0.0
    ).astype(bf16)
    keeps = 1.0 - jnp.sum(slot_hot, axis=1, keepdims=True)
    same = lax.broadcasted_iota(jnp.int32, (atoms, rows), 0) == lax.broadcasted_iota(
        jnp.int32, (atoms, rows), 1
    )
    slot_hot = slot_hot.astype(bf16)
    source = (dot(slot_hot, from_hot, NT) + jnp.where(same, keeps, 0.0)).astype(bf16)
    mfeat_ref[...] = dot(source, feats[...]).astype(bf16)
    entry = lax.broadcasted_iota(jnp.int32, (8, 6 * moves), 1) // moves
    along_row = lax.broadcasted_iota(jnp.int32, (8, 6 * moves), 0)
    move_shift = jnp.where(
        entry == 2 * along_row, -cell_edge, jnp.where(entry == 2 * along_row + 1, cell_edge, 0.0)
    ).astype(bf16)
    moved = dot(places_all, source, NT) + dot(move_shift, slot_hot, NT)
    mpos_ref[...] = moved[0:3, :].astype(bf16)
    mfeat_copy = pltpu.make_async_copy(mfeat_ref, mfeat_hbm, store_sem.at[1])
    mfeat_copy.start()
    mpos_copy = pltpu.make_async_copy(mpos_ref, mpos_hbm, store_sem.at[2])
    mpos_copy.start()

    for s, copy in enumerate(grad_copies):
        copy.wait_recv()
        gradient = gradient + grad_rx[s, :, 0:atoms]
    for a in range(3):
        force_ref[a] = -gradient[a : a + 1, :]
    force_copy = pltpu.make_async_copy(force_ref, force_hbm, store_sem.at[3])
    force_copy.start()
    for copy in small_copies + feat_copies + grad_copies:
        copy.wait_send()
    for copy in (energy_copy, mfeat_copy, mpos_copy, force_copy):
        copy.wait()


def finish(*refs):
    count = (len(refs) - 1) // 3
    sem = refs[-1]
    loads, stores = [], []
    for q in range(count):
        held = refs[2 * count + q]
        loads.append(pltpu.make_async_copy(refs[q], held, sem.at[q]))
        stores.append(pltpu.make_async_copy(held, refs[count + q], sem.at[count + q]))
    for copy in loads:
        copy.start()
    for load, store in zip(loads, stores):
        load.wait()
        store.start()
    for copy in stores:
        copy.wait()


def shards(axes, *args):
    (
        positions,
        features,
        ghost_lists,
        move_lists,
        neighbours,
        w_self,
        w_pair,
        w_radial,
        w_mix,
        w_env,
        w_scal,
        w_upd,
        w_out,
    ) = args
    atoms = positions.shape[-1]
    width = features.shape[-1]
    count = len(slots_of(axes))
    anywhere = pl.BlockSpec(memory_space=pl.ANY)
    semaphores = pltpu.SemaphoreType.DMA((count,))
    operands = (
        positions.reshape(positions.shape[3:]),
        features.reshape(features.shape[3:]),
        ghost_lists.reshape(ghost_lists.shape[3:]),
        move_lists.reshape(move_lists.shape[3:]),
        neighbours.reshape(neighbours.shape[3:]),
        w_radial,
        w_env.T,
        w_scal,
        w_out.reshape(1, -1),
        w_self,
        w_pair,
        w_mix,
        w_upd,
    )
    results = (
        jax.ShapeDtypeStruct((3, 1, atoms), f32),
        jax.ShapeDtypeStruct((1, atoms), f32),
        jax.ShapeDtypeStruct((3, atoms), bf16),
        jax.ShapeDtypeStruct((atoms, width), bf16),
    )
    found = pl.pallas_call(
        functools.partial(kernel, axes),
        out_shape=results,
        in_specs=[anywhere] * len(operands),
        out_specs=(anywhere,) * 4,
        scratch_shapes=[
            pltpu.VMEM(operands[q].shape, operands[q].dtype)
            for q in (0, 2, 3, 4, 5, 6, 7, 8, 9, 10, 11, 12)
        ]
        + [
            pltpu.VMEM((24, 128), f32),
            pltpu.VMEM((count, 24, 128), f32),
            pltpu.VMEM((atoms * (count + 1), width), bf16),
            pltpu.VMEM((count, 8, 128), f32),
            pltpu.VMEM((count, 8, 128), f32),
        ]
        + [pltpu.VMEM(result.shape, result.dtype) for result in results]
        + [
            pltpu.SemaphoreType.DMA((len(operands),)),
            pltpu.SemaphoreType.DMA((4,)),
        ]
        + [semaphores] * 6,
        compiler_params=pltpu.CompilerParams(
            collective_id=0, has_side_effects=True, vmem_limit_bytes=VMEM_BYTES
        ),
    )(*operands)
    forces, energy, moved_positions, moved_features = pl.pallas_call(
        finish,
        out_shape=results,
        in_specs=[anywhere] * 4,
        out_specs=(anywhere,) * 4,
        scratch_shapes=[pltpu.VMEM(result.shape, result.dtype) for result in results]
        + [pltpu.SemaphoreType.DMA((8,))],
    )(*found)
    return (
        forces.reshape(positions.shape),
        energy.reshape(1, 1, 1, atoms),
        moved_positions.reshape(positions.shape),
        moved_features.reshape(features.shape),
    )


def solution(mesh):
    axes = tuple((name, mesh.shape[name]) for name in ("gx", "gy", "gz"))
    cell = P("gx", "gy", "gz", None, None)
    lists = P("gx", "gy", "gz", None, None, None)
    return jax.shard_map(
        functools.partial(shards, axes),
        mesh=mesh,
        in_specs=(cell, cell, lists, lists, cell) + (P(),) * 8,
        out_specs=(cell, P("gx", "gy", "gz", None), cell, cell),
        check_vma=False,
    )
```
